32 devices in a mesh: tm: 4 (over x, core), cols: 8 (over z, y).
Axes of the slice: x: 2, y: 2, z: 4, core: 2. Of those that a mesh axis runs over, the one named last changes fastest.
Arguments:
- inv_diag: bfloat16 [4, 2048, 2048], P('tm', 'cols'), as said below
- sub_diag: bfloat16 [4, 2048, 2048], P('tm', 'cols'), may hold values from -0.09375 to 0.09375
- rhs: bfloat16 [4, 2048, 4096], P('tm', None, 'cols'), may hold values from -6 to 6
- carry_in: bfloat16 [2048, 4096], P(None, 'cols'), may hold values from -6 to 6
Outputs:
- solved: float32 [4, 2048, 4096], P('tm', None, 'cols')
The draws below stay inside these ranges and needn't reach their ends.
Inputs may be any that keep to these rules, and one draw needn't show every extreme that they name: Each block of inv_diag is lower triangular with diagonal entries between 0.5 and 1.5.
All inputs are finite; a program needn't handle non-finite values.
Results may differ from the reference program's by a relative error of at most 0.007.
Values may be sent and summed in bfloat16 or wider, within the bound.
A program may use at most 128 MiB of HBM per device.

```python
import jax
import jax.numpy as jnp
from jax import lax

BLOCK = 2048
BLOCKS = 4
SAMPLES = 4096


def draw_inv_diag(key, part):
    key_off = jax.random.fold_in(key, 11)
    key_diag = jax.random.fold_in(key, 12)
    spread_part = jax.random.normal(key_off, (BLOCKS, BLOCK, BLOCK), jnp.float32)
    diag_part = jax.random.uniform(key_diag, (BLOCKS, BLOCK), jnp.float32, 0.5, 1.5)
    spread_part = spread_part * (0.7 / jnp.sqrt(jnp.float32(BLOCK)))
    row_ids = lax.broadcasted_iota(jnp.int32, (BLOCK, BLOCK), 0)
    col_ids = lax.broadcasted_iota(jnp.int32, (BLOCK, BLOCK), 1)
    below_diag = jnp.where(row_ids > col_ids, spread_part, 0.0)
    on_diag = jnp.where(row_ids == col_ids, diag_part[:, :, None], 0.0)
    return (below_diag + on_diag).astype(jnp.bfloat16)


def levels(rng, shape, shards, low, high):
    def one(dim, shards_of):
        steps = jax.random.uniform(jax.random.fold_in(jax.random.fold_in(rng, 6), dim), (shards_of,), jnp.float32, low / len(shards), high / len(shards))
        return jnp.repeat(jnp.exp(steps), shape[dim] // shards_of).reshape((-1,) + (1,) * (len(shape) - dim - 1))

    gain = one(*shards[0])
    for cut in shards[1:]:
        gain = gain * one(*cut)
    return gain


def centred(rng, dims, scale, most, cuts=(), held_as=jnp.bfloat16):
    level = levels(rng, dims, cuts, -0.22, 0.18) if cuts else 1.0
    values = jax.random.normal(rng, dims, jnp.float32) * scale * level
    return jnp.minimum(jnp.maximum(values, -most), most).astype(held_as)


def setup_inputs(seed: int = 0) -> dict:
    keys = jax.random.split(jax.random.key(seed), 5)
    return {
        "inv_diag": draw_inv_diag(jax.random.fold_in(keys[4], 71), 0),
        "sub_diag": centred(keys[1], (BLOCKS, BLOCK, BLOCK), (2 * BLOCK) ** -0.5, 0.09375, ((0, 4), (1, 8))),
        "rhs": centred(keys[2], (BLOCKS, BLOCK, SAMPLES), 1.0, 6.0, ((0, 4), (2, 8))),
        "carry_in": centred(keys[3], (BLOCK, SAMPLES), 1.0, 6.0, ((1, 8),)),
    }


def advance(previous, inputs):
    inv_blk, sub_blk, source = inputs
    coupled = jnp.dot(sub_blk, previous, preferred_element_type=jnp.float32)
    update = (source.astype(jnp.float32) - coupled).astype(jnp.bfloat16)
    result = jnp.dot(inv_blk, update, preferred_element_type=jnp.float32)
    return result.astype(jnp.bfloat16), result


def reference(inv_diag, sub_diag, rhs, carry_in):
    final_block, solved = lax.scan(advance, carry_in, (inv_diag, sub_diag, rhs))
    return solved
```

```python
import functools

import jax
import jax.numpy as jnp
from jax import lax
from jax.experimental import pallas as pl
from jax.experimental.pallas import tpu as pltpu
from jax.sharding import PartitionSpec as P

MESH = pl.DeviceIdType.MESH
WIDE = 512
BATCH = 256
UP, DOWN, ACROSS = 0, 1, 2


def kernel(sections, lines, inv_ref, sub_ref, rhs_ref, carry_ref, out_ref,
           factors, rhs, prior, update, solved, rounded,
           own_sem, load_sem, store_sem, send_sem, recv_sem, prior_send, prior_recv):
    section = lax.axis_index("tm")
    col = lax.axis_index("cols")
    z, y = col // 2, lax.rem(col, 2)
    rows = inv_ref.shape[1]
    order = inv_ref.shape[2]
    pieces = order // WIDE
    batches = rhs_ref.shape[2] // BATCH

    own_rows = pl.ds(pl.multiple_of(col * rows, rows), rows)
    own = [
        pltpu.make_async_copy(sub_ref.at[0], factors.at[0, own_rows, :], own_sem.at[0]),
        pltpu.make_async_copy(inv_ref.at[0], factors.at[1, own_rows, :], own_sem.at[1]),
    ]
    for copy in own:
        copy.start()
    loads = [pltpu.make_async_copy(rhs_ref.at[0], rhs, load_sem.at[0])]
    carries = [
        pltpu.make_async_copy(carry_ref.at[:, pl.ds(b * BATCH, BATCH)], prior.at[b], load_sem.at[1 + b])
        for b in range(batches)
    ]

    barrier = pltpu.get_barrier_semaphore()

    def greet(cond, device):
        @pl.when(cond)
        def _():
            pl.semaphore_signal(barrier, inc=1, device_id=device, device_id_type=MESH)

    greet(z > 0, {"cols": col - 2})
    greet(z < lines - 1, {"cols": col + 2})
    pl.semaphore_signal(barrier, inc=1, device_id={"cols": 2 * z + 1 - y}, device_id_type=MESH)
    greet(section > 0, {"tm": section - 1})
    greet(section < sections - 1, {"tm": section + 1})
    ends = [z > 0, z < lines - 1, section > 0, section < sections - 1]
    pl.semaphore_wait(barrier, 1 + sum(jnp.where(end, 1, 0) for end in ends))

    def blocks(arr, z0):
        return pieces if arr == 0 else (z0 * 2 * rows) // WIDE + 1

    def piece(arr, z0, y0, j):
        c = 2 * z0 + y0
        return factors.at[arr, pl.ds(pl.multiple_of(c * rows, rows), rows),
                          pl.ds(pl.multiple_of(j * WIDE, WIDE), WIDE)]

    def remote(way, arr, z0, y0, j):
        c = 2 * z0 + y0
        ref = piece(arr, z0, y0, j)
        to = {UP: col + 2, DOWN: col - 2, ACROSS: 2 * z + 1 - y}[way]
        return pltpu.make_async_remote_copy(
            src_ref=ref, dst_ref=ref, send_sem=send_sem.at[way, arr, c, j],
            recv_sem=recv_sem.at[arr, c, j], device_id={"cols": to}, device_id_type=MESH)

    def if_(cond, fn):
        pl.when(cond)(fn)

    def each(count, fn):
        def body(j, carry):
            fn(j)
            return carry
        lax.fori_loop(0, count, body, 0)

    def line(arr, act, received):
        def own_piece(j):
            if_(z < lines - 1, lambda: act(remote(UP, arr, z, y, j)))
            if_(z > 0, lambda: act(remote(DOWN, arr, z, y, j)))
            act(remote(ACROSS, arr, z, y, j))
        each(blocks(arr, z), own_piece)

        def hop(d, carry):
            def from_below(j):
                received(arr, z - d, y, j)
                if_(z < lines - 1, lambda: act(remote(UP, arr, z - d, y, j)))
                act(remote(ACROSS, arr, z - d, y, j))

            def from_above(j):
                received(arr, z + d, y, j)
                if_(z > 0, lambda: act(remote(DOWN, arr, z + d, y, j)))
                act(remote(ACROSS, arr, z + d, y, j))

            if_(z - d >= 0, lambda: each(blocks(arr, z - d), from_below))
            if_(z + d < lines, lambda: each(blocks(arr, z + d), from_above))
            return carry
        lax.fori_loop(1, lines, hop, 0)

    def received(arr, z0, y0, j):
        remote(ACROSS, arr, z0, y0, j).wait_recv()

    for arr in range(2):
        own[arr].wait()
        if arr == 0:
            loads[0].start()

            @pl.when(section == 0)
            def _():
                for copy in carries:
                    copy.start()
        line(arr, lambda copy: copy.start(), received)

    def across(arr):
        def from_line(z0, carry):
            each(blocks(arr, z0), lambda j: received(arr, z0, 1 - y, j))
            return carry
        lax.fori_loop(0, lines, from_line, 0)

    across(0)
    across(1)

    loads[0].wait()

    @pl.when(section == 0)
    def _():
        for copy in carries:
            copy.wait()

    def handed(b, i):
        span = pl.ds(i * WIDE, WIDE)
        return pltpu.make_async_remote_copy(
            src_ref=rounded.at[b, span, :], dst_ref=prior.at[b, span, :],
            send_sem=prior_send.at[b, i], recv_sem=prior_recv.at[b, i],
            device_id={"tm": section + 1}, device_id_type=MESH)

    def stored(b, i):
        span = pl.ds(i * WIDE, WIDE)
        return pltpu.make_async_copy(
            solved.at[b, span, :], out_ref.at[0, span, pl.ds(b * BATCH, BATCH)], store_sem.at[b, i])

    for b in range(batches):
        @pl.when(section > 0)
        def _():
            for i in range(pieces):
                handed(b, i).wait_recv()

        for i in range(pieces):
            span = pl.ds(i * WIDE, WIDE)
            coupled = jnp.dot(factors[0, span, :], prior[b], preferred_element_type=jnp.float32)
            source = rhs[span, pl.ds(b * BATCH, BATCH)].astype(jnp.float32)
            update[span, :] = (source - coupled).astype(jnp.bfloat16)
        for i in range(pieces):
            span = pl.ds(i * WIDE, WIDE)
            known = (i + 1) * WIDE
            result = jnp.dot(factors[1, span, :known], update[:known, :], preferred_element_type=jnp.float32)
            solved[b, span, :] = result
            rounded[b, span, :] = result.astype(jnp.bfloat16)
            stored(b, i).start()
            if_(section < sections - 1, lambda: handed(b, i).start())

    for arr in range(2):
        line(arr, lambda copy: copy.wait_send(), lambda *_: None)
    for b in range(batches):
        for i in range(pieces):
            stored(b, i).wait()
            if_(section < sections - 1, lambda: handed(b, i).wait_send())


def shards(sections, cols, inv_diag, sub_diag, rhs, carry_in):
    order, samples = carry_in.shape
    batches, pieces = samples // BATCH, order // WIDE
    flops = 4 * order * order * samples
    return pl.pallas_call(
        functools.partial(kernel, sections, cols // 2),
        out_shape=jax.ShapeDtypeStruct(rhs.shape, jnp.float32),
        in_specs=[pl.BlockSpec(memory_space=pl.ANY)] * 4,
        out_specs=pl.BlockSpec(memory_space=pl.ANY),
        scratch_shapes=[
            pltpu.VMEM((2, order, order), jnp.bfloat16),
            pltpu.VMEM((order, samples), jnp.bfloat16),
            pltpu.VMEM((batches, order, BATCH), jnp.bfloat16),
            pltpu.VMEM((order, BATCH), jnp.bfloat16),
            pltpu.VMEM((batches, order, BATCH), jnp.float32),
            pltpu.VMEM((batches, order, BATCH), jnp.bfloat16),
            pltpu.SemaphoreType.DMA((2,)),
            pltpu.SemaphoreType.DMA((1 + batches,)),
            pltpu.SemaphoreType.DMA((batches, pieces)),
            pltpu.SemaphoreType.DMA((3, 2, cols, pieces)),
            pltpu.SemaphoreType.DMA((2, cols, pieces)),
            pltpu.SemaphoreType.DMA((batches, pieces)),
            pltpu.SemaphoreType.DMA((batches, pieces)),
        ],
        compiler_params=pltpu.CompilerParams(
            collective_id=0, has_side_effects=True, vmem_limit_bytes=48 * 1024 * 1024),
        cost_estimate=pl.CostEstimate(flops=flops, bytes_accessed=10 * order * samples, transcendentals=0),
    )(inv_diag, sub_diag, rhs, carry_in)


def solution(mesh):
    in_specs = (
        P("tm", "cols", None),
        P("tm", "cols", None),
        P("tm", None, "cols"),
        P(None, "cols"),
    )
    out_specs = P("tm", None, "cols")
    body = functools.partial(shards, mesh.shape["tm"], mesh.shape["cols"])
    return jax.shard_map(body, mesh=mesh, in_specs=in_specs, out_specs=out_specs, check_vma=False)
```

```python
import functools

import jax
import jax.numpy as jnp
from jax import lax
from jax.experimental import pallas as pl
from jax.experimental.pallas import tpu as pltpu
from jax.sharding import PartitionSpec as P

MESH = pl.DeviceIdType.MESH
WIDE = 512
BATCH = 256
UP, DOWN, ACROSS = 0, 1, 2
TURN = 1


def kernel(sections, lines, inv_ref, sub_ref, rhs_ref, carry_ref, out_ref,
           factors, rhs, prior, update, solved, rounded,
           own_sem, load_sem, store_sem, send_sem, recv_sem, prior_send, prior_recv, turn_sem):
    section = lax.axis_index("tm")
    col = lax.axis_index("cols")
    z, y = col // 2, lax.rem(col, 2)
    rows = inv_ref.shape[1]
    order = inv_ref.shape[2]
    pieces = order // WIDE
    batches = rhs_ref.shape[2] // BATCH

    own_rows = pl.ds(pl.multiple_of(col * rows, rows), rows)
    own = [
        pltpu.make_async_copy(sub_ref.at[0], factors.at[0, own_rows, :], own_sem.at[0]),
        pltpu.make_async_copy(inv_ref.at[0], factors.at[1, own_rows, :], own_sem.at[1]),
    ]
    for copy in own:
        copy.start()
    loads = [pltpu.make_async_copy(rhs_ref.at[0], rhs, load_sem.at[0])]
    carries = [
        pltpu.make_async_copy(carry_ref.at[:, pl.ds(b * BATCH, BATCH)], prior.at[:, pl.ds(b * BATCH, BATCH)], load_sem.at[1 + b])
        for b in range(batches)
    ]

    barrier = pltpu.get_barrier_semaphore()

    def greet(cond, device):
        @pl.when(cond)
        def _():
            pl.semaphore_signal(barrier, inc=1, device_id=device, device_id_type=MESH)

    greet(z > 0, {"cols": col - 2})
    greet(z < lines - 1, {"cols": col + 2})
    pl.semaphore_signal(barrier, inc=1, device_id={"cols": 2 * z + 1 - y}, device_id_type=MESH)
    greet(section > 0, {"tm": section - 1})
    greet(section < sections - 1, {"tm": section + 1})
    ends = [z > 0, z < lines - 1, section > 0, section < sections - 1]
    pl.semaphore_wait(barrier, 1 + sum(jnp.where(end, 1, 0) for end in ends))

    def blocks(arr, z0):
        return pieces if arr == 0 else (z0 * 2 * rows) // WIDE + 1

    def piece(arr, z0, y0, j):
        c = 2 * z0 + y0
        return factors.at[arr, pl.ds(pl.multiple_of(c * rows, rows), rows),
                          pl.ds(pl.multiple_of(j * WIDE, WIDE), WIDE)]

    def remote(way, arr, z0, y0, j):
        c = 2 * z0 + y0
        ref = piece(arr, z0, y0, j)
        to = {UP: col + 2, DOWN: col - 2, ACROSS: 2 * z + 1 - y}[way]
        return pltpu.make_async_remote_copy(
            src_ref=ref, dst_ref=ref, send_sem=send_sem.at[way, arr, c, j],
            recv_sem=recv_sem.at[arr, c, j], device_id={"cols": to}, device_id_type=MESH)

    def if_(cond, fn):
        pl.when(cond)(fn)

    def each(count, fn):
        def body(j, carry):
            fn(j)
            return carry
        lax.fori_loop(0, count, body, 0)

    last = pieces - 1
    early = 2 * rows == WIDE and sections > 2

    def nth(arr, j):
        return lax.rem(j + last, pieces) if arr == 0 else j

    def along(arr, act, arrive, z0, y0, j, up, down):
        arrive(arr, z0, y0, j)
        if up:
            if_(z < lines - 1, lambda: act(remote(UP, arr, z0, y0, j)))
        if down:
            if_(z > 0, lambda: act(remote(DOWN, arr, z0, y0, j)))

    def line(arr, act, arrive, between=lambda d: None):
        def own_piece(k):
            j = nth(arr, k)
            act(remote(ACROSS, arr, z, y, j))
            along(arr, act, lambda *_: None, z, y, j, True, True)
        each(blocks(arr, z), own_piece)
        if arr == 0:
            along(arr, act, arrive, z, 1 - y, last, True, True)
        between(0)

        def from_side(z0, up):
            def one(k):
                j = nth(arr, k)
                along(arr, act, arrive, z0, y, j, up, not up)
                if arr == 0:
                    if_(j != last, lambda: act(remote(ACROSS, arr, z0, y, j)))
                else:
                    act(remote(ACROSS, arr, z0, y, j))
            each(blocks(arr, z0), one)
            if arr == 0:
                along(arr, act, arrive, z0, 1 - y, last, up, not up)

        def hop(d, carry):
            if_(z - d >= 0, lambda: from_side(z - d, True))
            if_(z + d < lines, lambda: from_side(z + d, False))
            return carry

        if early:
            for d in range(1, lines):
                hop(d, 0)
                between(d)
        else:
            lax.fori_loop(1, lines, hop, 0)

    def received(arr, z0, y0, j):
        remote(ACROSS, arr, z0, y0, j).wait_recv()

    def across(arr):
        def from_line(z0, carry):
            each(last if arr == 0 else blocks(arr, z0), lambda j: received(arr, z0, 1 - y, j))
            return carry
        lax.fori_loop(0, lines, from_line, 0)

    def handed(b, i):
        ref = (pl.ds(i * WIDE, WIDE), pl.ds(b * BATCH, BATCH))
        return pltpu.make_async_remote_copy(
            src_ref=rounded.at[ref], dst_ref=prior.at[ref],
            send_sem=prior_send.at[b, i], recv_sem=prior_recv.at[b, i],
            device_id={"tm": section + 1}, device_id_type=MESH)

    def stored(b, i):
        ref = (pl.ds(i * WIDE, WIDE), pl.ds(b * BATCH, BATCH))
        return pltpu.make_async_copy(solved.at[ref], out_ref.at[0].at[ref], store_sem.at[b, i])

    def couple(i, cols):
        span = pl.ds(i * WIDE, WIDE)
        coupled = jnp.dot(factors[0, span, :], prior[:, cols], preferred_element_type=jnp.float32)
        update[span, cols] = (rhs[span, cols].astype(jnp.float32) - coupled).astype(jnp.bfloat16)

    def solve(i, cols, parts):
        span = pl.ds(i * WIDE, WIDE)
        known = (i + 1) * WIDE
        result = jnp.dot(factors[1, span, :known], update[:known, cols], preferred_element_type=jnp.float32)
        rounded[span, cols] = result.astype(jnp.bfloat16)
        for b in parts:
            if_(section < sections - 1, lambda: handed(b, i).start())
        solved[span, cols] = result
        for b in parts:
            stored(b, i).start()

    whole = pl.ds(0, batches * BATCH)

    def solve_plane(z0):
        for i in range(pieces):
            @pl.when(z0 == i)
            def _():
                for j in range(i + 1):
                    received(1, i, 1 - y, j)
                solve(i, whole, range(batches))

    def between(d):
        @pl.when(section < 2)
        def _():
            if d == 0:
                @pl.when(section == 1)
                def _():
                    for b in range(batches):
                        for i in range(pieces):
                            handed(b, i).wait_recv()
                for i in range(pieces // 2):
                    couple(i, whole)
            elif d == 1:
                for i in range(pieces // 2, pieces):
                    couple(i, whole)
            elif d == 2:
                solve_plane(z)
            else:
                solve_plane(z - d + 2)
                solve_plane(z + d - 2)
        if d == TURN:
            @pl.when(section == 0)
            def _():
                pl.semaphore_signal(turn_sem, inc=1, device_id={"tm": section + 1}, device_id_type=MESH)

    own[0].wait()
    loads[0].start()

    @pl.when(section == 0)
    def _():
        for copy in carries:
            copy.start()
    if early:
        @pl.when(section == 1)
        def _():
            pl.semaphore_wait(turn_sem, 1)
    line(0, lambda copy: copy.start(), received)
    own[1].wait()
    loads[0].wait()

    @pl.when(section == 0)
    def _():
        for copy in carries:
            copy.wait()

    if early:
        def between_all(d):
            if d == 0:
                across(0)
            between(d)
        line(1, lambda copy: copy.start(), received, between_all)

        @pl.when(section < 2)
        def _():
            for d in (lines - 2, lines - 1):
                solve_plane(z - d)
                solve_plane(z + d)
    else:
        line(1, lambda copy: copy.start(), received)
        across(0)

    @pl.when(section >= (2 if early else 0))
    def _():
        across(1)
        for b in range(batches):
            @pl.when(section > 0)
            def _():
                for i in range(pieces):
                    handed(b, i).wait_recv()

            cols = pl.ds(b * BATCH, BATCH)
            for i in range(pieces):
                couple(i, cols)
            for i in range(pieces):
                solve(i, cols, (b,))

    for arr in range(2):
        line(arr, lambda copy: copy.wait_send(), lambda *_: None)
    for b in range(batches):
        for i in range(pieces):
            stored(b, i).wait()
            if_(section < sections - 1, lambda: handed(b, i).wait_send())


def shards(sections, cols, inv_diag, sub_diag, rhs, carry_in):
    order, samples = carry_in.shape
    batches, pieces = samples // BATCH, order // WIDE
    flops = 4 * order * order * samples
    return pl.pallas_call(
        functools.partial(kernel, sections, cols // 2),
        out_shape=jax.ShapeDtypeStruct(rhs.shape, jnp.float32),
        in_specs=[pl.BlockSpec(memory_space=pl.ANY)] * 4,
        out_specs=pl.BlockSpec(memory_space=pl.ANY),
        scratch_shapes=[
            pltpu.VMEM((2, order, order), jnp.bfloat16),
            pltpu.VMEM((order, samples), jnp.bfloat16),
            pltpu.VMEM((order, samples), jnp.bfloat16),
            pltpu.VMEM((order, samples), jnp.bfloat16),
            pltpu.VMEM((order, samples), jnp.float32),
            pltpu.VMEM((order, samples), jnp.bfloat16),
            pltpu.SemaphoreType.DMA((2,)),
            pltpu.SemaphoreType.DMA((1 + batches,)),
            pltpu.SemaphoreType.DMA((batches, pieces)),
            pltpu.SemaphoreType.DMA((3, 2, cols, pieces)),
            pltpu.SemaphoreType.DMA((2, cols, pieces)),
            pltpu.SemaphoreType.DMA((batches, pieces)),
            pltpu.SemaphoreType.DMA((batches, pieces)),
            pltpu.SemaphoreType.REGULAR,
        ],
        compiler_params=pltpu.CompilerParams(
            collective_id=0, has_side_effects=True, vmem_limit_bytes=48 * 1024 * 1024),
        cost_estimate=pl.CostEstimate(flops=flops, bytes_accessed=10 * order * samples, transcendentals=0),
    )(inv_diag, sub_diag, rhs, carry_in)


def solution(mesh):
    in_specs = (
        P("tm", "cols", None),
        P("tm", "cols", None),
        P("tm", None, "cols"),
        P(None, "cols"),
    )
    out_specs = P("tm", None, "cols")
    body = functools.partial(shards, mesh.shape["tm"], mesh.shape["cols"])
    return jax.shard_map(body, mesh=mesh, in_specs=in_specs, out_specs=out_specs, check_vma=False)
```

```python
import functools

import jax
import jax.numpy as jnp
from jax import lax
from jax.experimental import pallas as pl
from jax.experimental.pallas import tpu as pltpu
from jax.sharding import PartitionSpec as P

MESH = pl.DeviceIdType.MESH
WIDE = 512
BATCH = 256
UP, DOWN, ACROSS = 0, 1, 2
TURN = 0


def kernel(sections, lines, inv_ref, sub_ref, rhs_ref, carry_ref, out_ref,
           factors, rhs, prior, update, solved, rounded,
           own_sem, load_sem, store_sem, send_sem, recv_sem, prior_send, prior_recv, turn_sem):
    section = lax.axis_index("tm")
    col = lax.axis_index("cols")
    z, y = col // 2, lax.rem(col, 2)
    rows = inv_ref.shape[1]
    order = inv_ref.shape[2]
    pieces = order // WIDE
    batches = rhs_ref.shape[2] // BATCH

    own_rows = pl.ds(pl.multiple_of(col * rows, rows), rows)
    own = [
        pltpu.make_async_copy(sub_ref.at[0], factors.at[0, own_rows, :], own_sem.at[0]),
        pltpu.make_async_copy(inv_ref.at[0], factors.at[1, own_rows, :], own_sem.at[1]),
    ]
    for copy in own:
        copy.start()
    loads = [pltpu.make_async_copy(rhs_ref.at[0], rhs, load_sem.at[0])]
    carries = [
        pltpu.make_async_copy(carry_ref.at[:, pl.ds(b * BATCH, BATCH)], prior.at[:, pl.ds(b * BATCH, BATCH)], load_sem.at[1 + b])
        for b in range(batches)
    ]

    barrier = pltpu.get_barrier_semaphore()

    def greet(cond, device):
        @pl.when(cond)
        def _():
            pl.semaphore_signal(barrier, inc=1, device_id=device, device_id_type=MESH)

    greet(z > 0, {"cols": col - 2})
    greet(z < lines - 1, {"cols": col + 2})
    pl.semaphore_signal(barrier, inc=1, device_id={"cols": 2 * z + 1 - y}, device_id_type=MESH)
    greet(section > 0, {"tm": section - 1})
    greet(section < sections - 1, {"tm": section + 1})
    ends = [z > 0, z < lines - 1, section > 0, section < sections - 1]
    pl.semaphore_wait(barrier, 1 + sum(jnp.where(end, 1, 0) for end in ends))

    def blocks(arr, z0):
        return pieces if arr == 0 else (z0 * 2 * rows) // WIDE + 1

    def piece(arr, z0, y0, j):
        c = 2 * z0 + y0
        return factors.at[arr, pl.ds(pl.multiple_of(c * rows, rows), rows),
                          pl.ds(pl.multiple_of(j * WIDE, WIDE), WIDE)]

    def remote(way, arr, z0, y0, j):
        c = 2 * z0 + y0
        ref = piece(arr, z0, y0, j)
        to = {UP: col + 2, DOWN: col - 2, ACROSS: 2 * z + 1 - y}[way]
        return pltpu.make_async_remote_copy(
            src_ref=ref, dst_ref=ref, send_sem=send_sem.at[way, arr, c, j],
            recv_sem=recv_sem.at[arr, c, j], device_id={"cols": to}, device_id_type=MESH)

    def if_(cond, fn):
        pl.when(cond)(fn)

    def each(count, fn):
        def body(j, carry):
            fn(j)
            return carry
        lax.fori_loop(0, count, body, 0)

    last = pieces - 1
    early = 2 * rows == WIDE and sections > 2

    def nth(arr, j):
        return lax.rem(j + last, pieces) if arr == 0 else j

    def along(arr, act, arrive, z0, y0, j, up, down):
        arrive(arr, z0, y0, j)
        if up:
            if_(z < lines - 1, lambda: act(remote(UP, arr, z0, y0, j)))
        if down:
            if_(z > 0, lambda: act(remote(DOWN, arr, z0, y0, j)))

    def line(arr, act, arrive, between=lambda d: None):
        def own_piece(k):
            j = nth(arr, k)
            act(remote(ACROSS, arr, z, y, j))
            along(arr, act, lambda *_: None, z, y, j, True, True)
        each(blocks(arr, z), own_piece)
        if arr == 0:
            along(arr, act, arrive, z, 1 - y, last, True, True)
        between(0)

        def from_side(z0, up):
            def one(k):
                j = nth(arr, k)
                along(arr, act, arrive, z0, y, j, up, not up)
                if arr == 0:
                    if_(j != last, lambda: act(remote(ACROSS, arr, z0, y, j)))
                else:
                    act(remote(ACROSS, arr, z0, y, j))
            each(blocks(arr, z0), one)
            if arr == 0:
                along(arr, act, arrive, z0, 1 - y, last, up, not up)

        def hop(d, carry):
            if_(z - d >= 0, lambda: from_side(z - d, True))
            if_(z + d < lines, lambda: from_side(z + d, False))
            return carry

        if early:
            for d in range(1, lines):
                hop(d, 0)
                between(d)
        else:
            lax.fori_loop(1, lines, hop, 0)

    def received(arr, z0, y0, j):
        remote(ACROSS, arr, z0, y0, j).wait_recv()

    def across(arr):
        def from_line(z0, carry):
            each(last if arr == 0 else blocks(arr, z0), lambda j: received(arr, z0, 1 - y, j))
            return carry
        lax.fori_loop(0, lines, from_line, 0)

    def rows_of(i):
        return pl.ds(i * WIDE if isinstance(i, int) else pl.multiple_of(i * WIDE, WIDE), WIDE)

    def handed(b, i):
        ref = (rows_of(i), pl.ds(b * BATCH, BATCH))
        return pltpu.make_async_remote_copy(
            src_ref=rounded.at[ref], dst_ref=prior.at[ref],
            send_sem=prior_send.at[b, i], recv_sem=prior_recv.at[b, i],
            device_id={"tm": section + 1}, device_id_type=MESH)

    def stored(b, i):
        ref = (pl.ds(i * WIDE, WIDE), pl.ds(b * BATCH, BATCH))
        return pltpu.make_async_copy(solved.at[ref], out_ref.at[0].at[ref], store_sem.at[b, i])

    def couple(i, cols):
        span = pl.ds(i * WIDE, WIDE)
        coupled = jnp.dot(factors[0, span, :], prior[:, cols], preferred_element_type=jnp.float32)
        update[span, cols] = (rhs[span, cols].astype(jnp.float32) - coupled).astype(jnp.bfloat16)

    def solve(i, cols, parts):
        span = pl.ds(i * WIDE, WIDE)
        known = (i + 1) * WIDE
        result = jnp.dot(factors[1, span, :known], update[:known, cols], preferred_element_type=jnp.float32)
        rounded[span, cols] = result.astype(jnp.bfloat16)
        for b in parts:
            if_(section < sections - 1, lambda: handed(b, i).start())
        solved[span, cols] = result
        for b in parts:
            stored(b, i).start()

    whole = pl.ds(0, batches * BATCH)

    def solve_plane(z0):
        for i in range(pieces):
            @pl.when(z0 == i)
            def _():
                for j in range(i + 1):
                    received(1, i, 1 - y, j)
                solve(i, whole, range(batches))

    def between(d):
        @pl.when(section < 2)
        def _():
            if d == 0:
                @pl.when(section == 1)
                def _():
                    for b in range(batches):
                        for i in range(pieces):
                            handed(b, i).wait_recv()
                for i in range(pieces // 2):
                    couple(i, whole)
            elif d == 1:
                for i in range(pieces // 2, pieces):
                    couple(i, whole)
            elif d == 2:
                solve_plane(z)
            else:
                solve_plane(z - d + 2)
                solve_plane(z + d - 2)
        if d == TURN:
            @pl.when(section == 0)
            def _():
                pl.semaphore_signal(turn_sem, inc=1, device_id={"tm": section + 1}, device_id_type=MESH)

    own[0].wait()
    loads[0].start()

    @pl.when(section == 0)
    def _():
        for copy in carries:
            copy.start()
    if early:
        @pl.when(section == 1)
        def _():
            pl.semaphore_wait(turn_sem, 1)
    line(0, lambda copy: copy.start(), received)
    own[1].wait()
    loads[0].wait()

    @pl.when(section == 0)
    def _():
        for copy in carries:
            copy.wait()

    if early:
        def between_all(d):
            if d == 0:
                across(0)
            between(d)
        line(1, lambda copy: copy.start(), received, between_all)

        @pl.when(section < 2)
        def _():
            for d in (lines - 2, lines - 1):
                solve_plane(z - d)
                solve_plane(z + d)
    else:
        line(1, lambda copy: copy.start(), received)
        across(0)

    @pl.when(section >= (2 if early else 0))
    def _():
        across(1)
        solved[...] = rhs[...].astype(jnp.float32)

        def add_group(g):
            @pl.when(section > 0)
            def _():
                for b in range(batches):
                    handed(b, g).wait_recv()
            group = pl.ds(pl.multiple_of(g * WIDE, WIDE), WIDE)
            for i in range(pieces):
                span = pl.ds(i * WIDE, WIDE)
                solved[span, :] -= jnp.dot(
                    factors[0, span, group], prior[group, :], preferred_element_type=jnp.float32)

        if early:
            first = jnp.where(section == 2, z, 0)
            add_group(first)

            def next_groups(d, carry):
                if_(first - d >= 0, lambda: add_group(first - d))
                if_(first + d < lines, lambda: add_group(first + d))
                return carry
            lax.fori_loop(1, lines, next_groups, 0)
        else:
            lax.fori_loop(0, pieces, lambda g, carry: (add_group(g), carry)[1], 0)
        for i in range(pieces):
            span = pl.ds(i * WIDE, WIDE)
            update[span, :] = solved[span, :].astype(jnp.bfloat16)
            solve(i, whole, range(batches))

    for arr in range(2):
        line(arr, lambda copy: copy.wait_send(), lambda *_: None)
    for b in range(batches):
        for i in range(pieces):
            stored(b, i).wait()
            if_(section < sections - 1, lambda: handed(b, i).wait_send())


def shards(sections, cols, inv_diag, sub_diag, rhs, carry_in):
    order, samples = carry_in.shape
    batches, pieces = samples // BATCH, order // WIDE
    flops = 4 * order * order * samples
    return pl.pallas_call(
        functools.partial(kernel, sections, cols // 2),
        out_shape=jax.ShapeDtypeStruct(rhs.shape, jnp.float32),
        in_specs=[pl.BlockSpec(memory_space=pl.ANY)] * 4,
        out_specs=pl.BlockSpec(memory_space=pl.ANY),
        scratch_shapes=[
            pltpu.VMEM((2, order, order), jnp.bfloat16),
            pltpu.VMEM((order, samples), jnp.bfloat16),
            pltpu.VMEM((order, samples), jnp.bfloat16),
            pltpu.VMEM((order, samples), jnp.bfloat16),
            pltpu.VMEM((order, samples), jnp.float32),
            pltpu.VMEM((order, samples), jnp.bfloat16),
            pltpu.SemaphoreType.DMA((2,)),
            pltpu.SemaphoreType.DMA((1 + batches,)),
            pltpu.SemaphoreType.DMA((batches, pieces)),
            pltpu.SemaphoreType.DMA((3, 2, cols, pieces)),
            pltpu.SemaphoreType.DMA((2, cols, pieces)),
            pltpu.SemaphoreType.DMA((batches, pieces)),
            pltpu.SemaphoreType.DMA((batches, pieces)),
            pltpu.SemaphoreType.REGULAR,
        ],
        compiler_params=pltpu.CompilerParams(
            collective_id=0, has_side_effects=True, vmem_limit_bytes=48 * 1024 * 1024),
        cost_estimate=pl.CostEstimate(flops=flops, bytes_accessed=10 * order * samples, transcendentals=0),
    )(inv_diag, sub_diag, rhs, carry_in)


def solution(mesh):
    in_specs = (
        P("tm", "cols", None),
        P("tm", "cols", None),
        P("tm", None, "cols"),
        P(None, "cols"),
    )
    out_specs = P("tm", None, "cols")
    body = functools.partial(shards, mesh.shape["tm"], mesh.shape["cols"])
    return jax.shard_map(body, mesh=mesh, in_specs=in_specs, out_specs=out_specs, check_vma=False)
```
